32 devices in a mesh: dp: 4 (over y, x), expert: 4 (over z), tensor: 2 (over core).
Axes of the slice: x: 2, y: 2, z: 4, core: 2. Of those that a mesh axis runs over, the one named last changes fastest.
Arguments:
- tokens: bfloat16 [1024, 6144], P(('dp', 'expert'), 'tensor'), may hold values from -6 to 6
- routes: int32 [1024, 2], P(('dp', 'expert')), may hold values from 0 to 3, all different within a row; in each aligned block of 64 rows (0 to 63, 64 to 127, ...) at most 34 rows name the same one
- route_weights: float32 [1024, 2], P(('dp', 'expert')), may hold values from 0.2 to 1
- gate_proj: bfloat16 [4, 6144, 8192], P('expert', 'dp', 'tensor'), may hold values from -0.078125 to 0.078125
- up_proj: bfloat16 [4, 6144, 8192], P('expert', 'dp', 'tensor'), may hold values from -0.078125 to 0.078125
- down_proj: bfloat16 [4, 8192, 6144], P('expert', 'tensor', 'dp'), may hold values from -0.0625 to 0.0625
Outputs:
- mixed: bfloat16 [1024, 6144], P(('dp', 'expert'), 'tensor')
The draws below stay inside these ranges and needn't reach their ends.
Inputs may be any that keep to these rules, and one draw needn't show every extreme that they name: `routes`: in each aligned block of 64 rows, no expert is named by more than 34 rows, a bound that some block reaches; a row names 2 different experts.
All inputs are finite; a program needn't handle non-finite values.
Results may differ from the reference program's by a relative error of at most 0.0066.
Values may be sent and summed in bfloat16 or wider, within the bound.
A program may use at most 256 MiB of HBM per device.

```python
import math
import jax
import jax.numpy as jnp
import numpy as np
from jax import lax

D = 6144
FF = 8192
TOPK = 2
TOK_DEV = 64
EXPERTS = 4
TOKENS = 1024
CAP = 34
FF_DEV = 4096
N_DP = 4
N_EXPERT = 4
N_TENSOR = 2


def shard_levels(own_key, shape, shards, least, largest):
    factor_of, own = 1.0, jax.random.fold_in(own_key, 6)
    for dim, blocks in shards:
        steps = jnp.exp(jax.random.uniform(jax.random.fold_in(own, dim), (blocks,), jnp.float32, least / len(shards), largest / len(shards)))
        factor_of = factor_of * jnp.repeat(steps, shape[dim] // blocks).reshape([-1 if axis == dim else 1 for axis in range(len(shape))])
    return factor_of


def assign_block(key, own, number, rows, number_of, top, bound, skew):
    sequence = jax.random.permutation(key, number_of)
    packed, ordinary = portions_of(number_of, rows * top, bound, skew, True), portions_of(number_of, rows * top, bound, skew, False)
    places = jnp.arange(number_of)

    def named(tallies, offset_by):
        used = int((tallies > 0).sum())
        fixed = max(1, used // 4)
        moved = fixed + (places - fixed + offset_by * (used - fixed)) % max(1, number_of - fixed)
        return jnp.zeros((number_of,), jnp.int32).at[sequence[jnp.where(places < fixed, places, moved)]].set(jnp.asarray(tallies, jnp.int32))

    tallies = jnp.where(number % 4 == 0, named(packed, number // 4), named(ordinary, number - number // 4 - 1))
    mixed = jax.random.permutation(jax.random.fold_in(own, 3), number_of)
    donor, taker = mixed[0:number_of // 2 * 2:2], mixed[1:number_of // 2 * 2:2]
    slack = jnp.minimum(tallies[donor] - 1, bound - tallies[taker]) // 2
    slack = jnp.where((donor == sequence[0]) | (taker == sequence[0]) | (tallies[taker] == 0), 0, jnp.maximum(slack, 0))
    moved = jax.random.randint(jax.random.fold_in(own, 4), (number_of // 2,), 0, 1 << 20) % (slack + 1)
    tallies = tallies.at[donor].add(-moved).at[taker].add(moved)
    items = jnp.searchsorted(jnp.cumsum(tallies), jnp.arange(rows * top), side="right").astype(jnp.int32)
    grid = items.reshape(top, rows).T
    grid = grid[jax.random.permutation(jax.random.fold_in(own, 1), rows)]
    offset_by = jax.random.randint(jax.random.fold_in(own, 2), (rows, 1), 0, top)
    return jnp.take_along_axis(grid, (jnp.arange(top)[None, :] + offset_by) % top, axis=1)


def portions_of(count, total, bound, slope, full):
    portions = [(1 << 20) // math.isqrt(rank ** slope) + 1 for rank in range(1, count + 1)]
    largest = bound if full else min(bound, max(-(-total // count), total * portions[0] // sum(portions)))
    least = 1 if total - largest >= count - 1 else 0
    given, rest = [largest] + [least] * (count - 1), total - largest - least * (count - 1)
    while rest > 0:
        candidates = [i for i in range(1, count) if given[i] < largest] or [i for i in range(1, count) if given[i] < bound]
        whole, budget = sum([portions[i] for i in candidates]), rest
        for i in candidates:
            more = min(bound - given[i], max(1, budget * portions[i] // whole), rest)
            given[i] = given[i] + more
            rest = rest - more
    return np.array(given)


def normal_values(own_key, shape, width, most, shards=(), held_as=jnp.bfloat16):
    drawn = jax.random.normal(own_key, shape, jnp.float32) * width
    if len(shards) > 0:
        drawn = shard_levels(own_key, shape, shards, -0.22, 0.18) * drawn
    return jnp.clip(drawn, min=-most, max=most).astype(held_as)


def setup_inputs(seed: int = 0) -> dict:
    arg_keys = jax.random.split(jax.random.key(seed), 7)
    tokens = normal_values(arg_keys[0], (TOKENS, D), 1.0, 6.0, ((0, 16), (1, 2)))
    routes_keys = jax.random.split(jax.random.fold_in(arg_keys[1], 1), TOKENS // TOK_DEV)
    routes_turns = jax.random.permutation(jax.random.fold_in(arg_keys[1], 3), TOKENS // TOK_DEV)
    routes = jax.vmap(lambda own, number: assign_block(jax.random.fold_in(arg_keys[1], 2), own, number, TOK_DEV, EXPERTS, TOPK, CAP, 2))(routes_keys, routes_turns).reshape((TOKENS, TOPK))
    route_weights = jnp.clip(0.2 + 0.8 * jax.random.uniform(arg_keys[2], (TOKENS, TOPK), jnp.float32) ** shard_levels(arg_keys[2], (TOKENS, TOPK), ((0, 16),), -0.2, 0.2), 0.2, 1.0)
    gate_proj = normal_values(arg_keys[3], (EXPERTS, D, FF), D ** -0.5, 0.078125, ((0, 4), (1, 4), (2, 2)))
    up_proj = normal_values(arg_keys[4], (EXPERTS, D, FF), D ** -0.5, 0.078125, ((0, 4), (1, 4), (2, 2)))
    down_proj = normal_values(arg_keys[5], (EXPERTS, FF, D), FF ** -0.5, 0.0625, ((0, 4), (1, 2), (2, 4)))
    return {"tokens": tokens, "routes": routes, "route_weights": route_weights, "gate_proj": gate_proj, "up_proj": up_proj, "down_proj": down_proj}


def reference(tokens, routes, route_weights, gate_proj, up_proj, down_proj):
    limit = N_DP * N_EXPERT * CAP
    flat_routes = routes.reshape(-1)
    flat_weights = route_weights.reshape(-1)

    def one_expert(expert):
        chosen = flat_routes == expert
        picks = jnp.nonzero(chosen, size=limit, fill_value=0)[0].astype(jnp.int32)
        live_slot = (jnp.arange(limit) < jnp.sum(chosen.astype(jnp.int32))).astype(jnp.float32)
        owners = (picks // TOPK).astype(jnp.int32)
        row_data = tokens[owners]
        gate = jnp.dot(row_data, gate_proj[expert], preferred_element_type=jnp.float32)
        up_val = jnp.dot(row_data, up_proj[expert], preferred_element_type=jnp.float32)
        hidden = (jax.nn.silu(gate) * up_val).astype(jnp.bfloat16)
        hidden_blocks = hidden.reshape(limit, N_TENSOR, FF_DEV)
        down_blocks = down_proj[expert].reshape(N_TENSOR, FF_DEV, D)

        def add_block(running, block_id):
            block_term = jnp.dot(hidden_blocks[:, block_id], down_blocks[block_id], preferred_element_type=jnp.float32)
            block_term = lax.optimization_barrier(block_term.astype(jnp.bfloat16)).astype(jnp.float32)
            return running + block_term, None

        running, _ = lax.scan(add_block, jnp.zeros((limit, D), jnp.float32), jnp.arange(N_TENSOR, dtype=jnp.int32))
        expert_out = lax.optimization_barrier(running.astype(jnp.bfloat16)).astype(jnp.float32)
        scaled = expert_out * (flat_weights[picks] * live_slot)[:, None]
        return owners, scaled

    owners, scaled = lax.map(one_expert, jnp.arange(EXPERTS, dtype=jnp.int32))
    mixed = jnp.zeros((TOKENS, D), jnp.float32).at[owners.reshape(-1)].add(scaled.reshape(-1, D))
    return mixed.astype(jnp.bfloat16)
```

```python
import jax
import jax.numpy as jnp
from jax import lax
from jax.sharding import PartitionSpec as P

TOPK = 2


def shards(tokens, routes, route_weights, gate_proj, up_proj, down_proj):
    n_tokens, part = tokens.shape
    n_experts = lax.axis_size("expert") * gate_proj.shape[0]
    n_dp, n_tensor = lax.axis_size("dp"), lax.axis_size("tensor")
    capacity = min(n_tokens, n_tokens * TOPK // n_experts + 2)
    n_slots = n_experts * capacity
    width = part * n_tensor // n_dp
    piece = width // n_tensor
    if n_dp % n_tensor == 0:
        spread = lax.all_to_all(
            tokens.reshape(n_tokens, n_dp // n_tensor, n_tensor, piece),
            "tensor", split_axis=2, concat_axis=1, tiled=True,
        )
        spread = spread.reshape(n_tokens, n_dp * piece)
    else:
        whole = lax.all_gather(tokens, "tensor", axis=1, tiled=True)
        whole = whole.reshape(n_tokens, n_dp, n_tensor, piece)
        spread = lax.dynamic_index_in_dim(whole, lax.axis_index("tensor"), 2, False)
        spread = spread.reshape(n_tokens, n_dp * piece)
    flat_routes = routes.reshape(-1)
    one_hot = (flat_routes[:, None] == jnp.arange(n_experts, dtype=jnp.int32)[None, :]).astype(
        jnp.int32
    )
    earlier = jnp.cumsum(one_hot, axis=0) - one_hot
    slot_index = jnp.sum(earlier * one_hot, axis=1)
    dest_slot = flat_routes * capacity + slot_index
    slots = jnp.arange(n_slots, dtype=jnp.int32)
    dest = dest_slot.reshape(n_tokens, TOPK)
    select = sum(
        (dest[:, k][None, :] == slots[:, None]).astype(jnp.bfloat16) for k in range(TOPK)
    )
    outgoing = jnp.dot(select, spread, preferred_element_type=jnp.float32).astype(jnp.bfloat16)
    received = lax.all_to_all(
        outgoing.reshape(n_experts, capacity, -1), "expert", split_axis=0, concat_axis=0, tiled=True
    )
    blocks = lax.all_to_all(
        received.reshape(n_slots, n_dp * piece), "dp", split_axis=1, concat_axis=0, tiled=True
    )
    rows = lax.all_gather(blocks, "tensor", axis=1, tiled=True)
    gate_part = jnp.dot(rows, gate_proj[0], preferred_element_type=jnp.float32)
    gate_sum = lax.psum_scatter(
        gate_part.astype(jnp.bfloat16), "dp", scatter_dimension=0, tiled=True
    ).astype(jnp.float32)
    up_part = jnp.dot(rows, up_proj[0], preferred_element_type=jnp.float32)
    up_sum = lax.psum_scatter(
        up_part.astype(jnp.bfloat16), "dp", scatter_dimension=0, tiled=True
    ).astype(jnp.float32)
    hidden = (jax.nn.silu(gate_sum) * up_sum).astype(jnp.bfloat16)
    hidden = lax.all_gather(hidden, "dp", axis=0, tiled=True)
    terms = jnp.dot(hidden, down_proj[0], preferred_element_type=jnp.float32)
    expert_rows = lax.psum_scatter(
        terms.astype(jnp.bfloat16), "tensor", scatter_dimension=1, tiled=True
    )
    back = lax.all_to_all(expert_rows, "dp", split_axis=0, concat_axis=1, tiled=True)
    returned = lax.all_to_all(
        back.reshape(n_experts, capacity, -1), "expert", split_axis=0, concat_axis=0, tiled=True
    ).reshape(n_slots, -1)
    picked = jnp.take(returned, dest_slot, axis=0).astype(jnp.float32)
    picked = picked.reshape(n_tokens, TOPK, -1)
    mixed = jnp.sum(picked * route_weights[:, :, None], axis=1).astype(jnp.bfloat16)
    if n_dp % n_tensor == 0:
        mixed = lax.all_to_all(
            mixed.reshape(n_tokens, n_tensor, n_dp // n_tensor, 1, piece),
            "tensor", split_axis=1, concat_axis=3, tiled=True,
        )
        return mixed.reshape(n_tokens, part)
    whole = lax.all_gather(mixed.reshape(n_tokens, n_dp, 1, piece), "tensor", axis=2, tiled=True)
    whole = whole.reshape(n_tokens, n_tensor, part)
    return lax.dynamic_index_in_dim(whole, lax.axis_index("tensor"), 1, False)


def solution(mesh):
    placed = (
        P(("dp", "expert"), "tensor"),
        P(("dp", "expert"), None),
        P(("dp", "expert"), None),
        P("expert", "dp", "tensor"),
        P("expert", "dp", "tensor"),
        P("expert", "tensor", "dp"),
    )
    return jax.shard_map(
        shards, mesh=mesh, in_specs=placed, out_specs=P(("dp", "expert"), "tensor"), check_vma=False
    )
```

```python
import functools

import jax
import jax.numpy as jnp
from jax import lax
from jax.experimental import pallas as pl
from jax.experimental.pallas import tpu as pltpu
from jax.sharding import PartitionSpec as P

TOPK = 2
CHUNK = 256
MESH = pl.DeviceIdType.MESH


def kernel(
    n_chunks, x_ref, wg_ref, wu_ref, wd_ref, out_ref,
    xs, wt, wd, snd1, rcv1, snd2, rcv2, hid, keep, acc, ysnd, yrcv,
    w_sem, wd_sem, x_sem, y_sem, s1, r1, s2, r2, hs, hr,
):
    me, ex, core = lax.axis_index("dp"), lax.axis_index("expert"), lax.axis_index("tensor")
    mx, my = me % 2, me // 2
    xn, yn, diag = my * 2 + 1 - mx, (1 - my) * 2 + mx, 3 - me
    to_x, to_y, to_core = (xn, ex, core), (yn, ex, core), (me, ex, 1 - core)
    half = x_ref.shape[1]
    owned = n_chunks * CHUNK
    owners = (diag, diag, xn, yn, yn, xn, me, me)

    def weight(k, c, slot):
        src = wg_ref if k % 2 == 0 else wu_ref
        cols = pl.ds(pl.multiple_of(owners[k] * owned + c * CHUNK, CHUNK), CHUNK)
        return pltpu.make_async_copy(src.at[:, cols], wt.at[slot, k], w_sem.at[slot, k])

    def remote(src, dst, send, recv, to):
        return pltpu.make_async_remote_copy(
            src_ref=src, dst_ref=dst, send_sem=send, recv_sem=recv,
            device_id=to, device_id_type=MESH,
        )

    def first(c, k):
        return remote(snd1.at[c, k], rcv1.at[c, k], s1.at[c, k], r1.at[c, k],
                      to_x if k % 2 == 0 else to_y)

    def second(c, k):
        return remote(snd2.at[c, k], rcv2.at[c, k], s2.at[c, k], r2.at[c, k],
                      to_y if k == 0 else to_x)

    def spread(c, k):
        if k == 0:
            return remote(hid.at[c, 0], hid.at[c, 1], hs.at[c, 0], hr.at[c, 0], to_x)
        if k == 1:
            return remote(hid.at[c, 0], hid.at[c, 2], hs.at[c, 1], hr.at[c, 1], to_y)
        cols = pl.ds((k - 2) * (CHUNK // 2), CHUNK // 2)
        return remote(hid.at[c, k - 1, :, cols], hid.at[c, 3, :, cols], hs.at[c, k],
                      hr.at[c, k], to_y if k == 2 else to_x)

    down_copy = pltpu.make_async_copy(wd_ref, wd, wd_sem)
    for k in range(8):
        weight(k, 0, 0).start()
    barrier = pltpu.get_barrier_semaphore()
    for to in (to_x, to_y, to_core):
        pl.semaphore_signal(barrier, inc=1, device_id=to, device_id_type=MESH)
    pl.semaphore_wait(barrier, 3)
    x_copy = remote(x_ref, xs.at[core], x_sem.at[0], x_sem.at[1], to_core)
    x_copy.start()
    xs[core] = x_ref[...]
    acc[...] = jnp.zeros_like(acc)
    x_copy.wait()

    def product(slot, k):
        return jnp.dot(
            xs[0], wt[slot, k, :half, :], preferred_element_type=jnp.float32
        ) + jnp.dot(xs[1], wt[slot, k, half:, :], preferred_element_type=jnp.float32)

    def step(i, carry):
        @pl.when(i < n_chunks)
        def _():
            c = jnp.minimum(i, n_chunks - 1)
            slot = c % 2

            @pl.when(c + 1 < n_chunks)
            def _():
                for k in range(8):
                    weight(k, c + 1, 1 - slot).start()

            @pl.when(c == 0)
            def _():
                down_copy.start()

            for k in range(4):
                weight(k, c, slot).wait()
                snd1[c, k] = product(slot, k).astype(jnp.bfloat16)
                first(c, k).start()
            for k in range(4, 8):
                weight(k, c, slot).wait()
                keep[slot, k - 4] = product(slot, k)

        @pl.when((i >= 2) & (i < n_chunks + 2))
        def _():
            c = i - 2
            for k in range(2):
                spread(c, k).wait_recv()
                spread(c, k + 2).start()

        @pl.when((i >= 1) & (i < n_chunks + 1))
        def _():
            c = i - 1
            for k in range(2):
                first(c, k).wait_recv()
                snd2[c, k] = (keep[c % 2, k] + rcv1[c, k].astype(jnp.float32)).astype(jnp.bfloat16)
                second(c, k).start()

        @pl.when(i >= 3)
        def _():
            c = i - 3

            @pl.when(c == 0)
            def _():
                down_copy.wait()

            spread(c, 2).wait_recv()
            spread(c, 3).wait_recv()
            for n in range(0, acc.shape[1], 512):
                total = acc[:, n : n + 512]
                for s, owner in enumerate((me, xn, yn, diag)):
                    at = pl.ds(pl.multiple_of(owner * owned + c * CHUNK, CHUNK), CHUNK)
                    total += jnp.dot(
                        hid[c, s], wd[at, n : n + 512], preferred_element_type=jnp.float32
                    )
                acc[:, n : n + 512] = total

        @pl.when((i >= 1) & (i < n_chunks + 1))
        def _():
            c = i - 1
            first(c, 2).wait_recv()
            first(c, 3).wait_recv()
            second(c, 0).wait_recv()
            second(c, 1).wait_recv()
            gate = keep[c % 2, 2] + rcv1[c, 2].astype(jnp.float32) + rcv2[c, 0].astype(jnp.float32)
            up = keep[c % 2, 3] + rcv1[c, 3].astype(jnp.float32) + rcv2[c, 1].astype(jnp.float32)
            hid[c, 0] = (gate / (1.0 + jnp.exp(-gate)) * up).astype(jnp.bfloat16)
            spread(c, 0).start()
            spread(c, 1).start()

        return carry

    lax.fori_loop(0, n_chunks + 3, step, 0)
    ysnd[0] = acc[:, :half].astype(jnp.bfloat16)
    ysnd[1] = acc[:, half:].astype(jnp.bfloat16)
    y_copy = remote(ysnd.at[1 - core], yrcv, y_sem.at[0], y_sem.at[1], to_core)
    y_copy.start()

    def drain(c, carry):
        for k in range(4):
            first(c, k).wait_send()
            spread(c, k).wait_send()
        for k in range(2):
            second(c, k).wait_send()
        return carry

    lax.fori_loop(0, n_chunks, drain, 0)
    y_copy.wait()
    out_ref[...] = (ysnd[core].astype(jnp.float32) + yrcv[...].astype(jnp.float32)).astype(
        jnp.bfloat16
    )


def experts(blocks, gate_proj, up_proj, down_proj):
    rows, half = blocks.shape
    width, ff = gate_proj.shape
    n_chunks = ff // (4 * CHUNK)
    vmem = pl.BlockSpec(memory_space=pltpu.VMEM)
    hbm = pl.BlockSpec(memory_space=pl.ANY)
    bf, dma = jnp.bfloat16, pltpu.SemaphoreType.DMA
    return pl.pallas_call(
        functools.partial(kernel, n_chunks),
        out_shape=jax.ShapeDtypeStruct((rows, half), bf),
        in_specs=[vmem, hbm, hbm, hbm],
        out_specs=vmem,
        scratch_shapes=[
            pltpu.VMEM((2, rows, half), bf),
            pltpu.VMEM((2, 8, width, CHUNK), bf),
            pltpu.VMEM((ff, width), bf),
            pltpu.VMEM((n_chunks, 4, rows, CHUNK), bf),
            pltpu.VMEM((n_chunks, 4, rows, CHUNK), bf),
            pltpu.VMEM((n_chunks, 2, rows, CHUNK), bf),
            pltpu.VMEM((n_chunks, 2, rows, CHUNK), bf),
            pltpu.VMEM((n_chunks, 4, rows, CHUNK), bf),
            pltpu.VMEM((2, 4, rows, CHUNK), jnp.float32),
            pltpu.VMEM((rows, width), jnp.float32),
            pltpu.VMEM((2, rows, half), bf),
            pltpu.VMEM((rows, half), bf),
            dma((2, 8)), dma, dma((2,)), dma((2,)),
            dma((n_chunks, 4)), dma((n_chunks, 4)),
            dma((n_chunks, 2)), dma((n_chunks, 2)),
            dma((n_chunks, 4)), dma((n_chunks, 4)),
        ],
        compiler_params=pltpu.CompilerParams(
            collective_id=0, has_side_effects=True, vmem_limit_bytes=63 * 1024 * 1024
        ),
        cost_estimate=pl.CostEstimate(
            flops=6 * rows * width * ff, bytes_accessed=6 * width * ff,
            transcendentals=rows * ff // 4,
        ),
    )(blocks, gate_proj, up_proj, down_proj)


def plain_experts(blocks, gate_proj, up_proj, down_proj):
    rows = lax.all_gather(blocks, "tensor", axis=1, tiled=True)
    gate_part = jnp.dot(rows, gate_proj[0], preferred_element_type=jnp.float32)
    gate_sum = lax.psum_scatter(
        gate_part, "dp", scatter_dimension=0, tiled=True
    ).astype(jnp.float32)
    up_part = jnp.dot(rows, up_proj[0], preferred_element_type=jnp.float32)
    up_sum = lax.psum_scatter(
        up_part, "dp", scatter_dimension=0, tiled=True
    ).astype(jnp.float32)
    hidden = (jax.nn.silu(gate_sum) * up_sum).astype(jnp.bfloat16)
    hidden = lax.all_gather(hidden, "dp", axis=0, tiled=True)
    terms = jnp.dot(hidden, down_proj[0], preferred_element_type=jnp.float32)
    expert_rows = lax.psum_scatter(
        terms.astype(jnp.bfloat16), "tensor", scatter_dimension=1, tiled=True
    )
    return expert_rows


def shards(tokens, routes, route_weights, gate_proj, up_proj, down_proj):
    n_tokens, part = tokens.shape
    n_experts = lax.axis_size("expert") * gate_proj.shape[0]
    n_dp, n_tensor = lax.axis_size("dp"), lax.axis_size("tensor")
    capacity = min(n_tokens, n_tokens * TOPK // n_experts + 2)
    n_slots = n_experts * capacity
    width = part * n_tensor // n_dp
    piece = width // n_tensor
    if n_dp % n_tensor == 0:
        spread = lax.all_to_all(
            tokens.reshape(n_tokens, n_dp // n_tensor, n_tensor, piece),
            "tensor", split_axis=2, concat_axis=1, tiled=True,
        )
        spread = spread.reshape(n_tokens, n_dp * piece)
    else:
        whole = lax.all_gather(tokens, "tensor", axis=1, tiled=True)
        whole = whole.reshape(n_tokens, n_dp, n_tensor, piece)
        spread = lax.dynamic_index_in_dim(whole, lax.axis_index("tensor"), 2, False)
        spread = spread.reshape(n_tokens, n_dp * piece)
    flat_routes = routes.reshape(-1)
    one_hot = (flat_routes[:, None] == jnp.arange(n_experts, dtype=jnp.int32)[None, :]).astype(
        jnp.int32
    )
    earlier = jnp.cumsum(one_hot, axis=0) - one_hot
    slot_index = jnp.sum(earlier * one_hot, axis=1)
    dest_slot = flat_routes * capacity + slot_index
    slots = jnp.arange(n_slots, dtype=jnp.int32)
    dest = dest_slot.reshape(n_tokens, TOPK)
    select = sum(
        (dest[:, k][None, :] == slots[:, None]).astype(jnp.bfloat16) for k in range(TOPK)
    )
    outgoing = jnp.dot(select, spread, preferred_element_type=jnp.float32).astype(jnp.bfloat16)
    received = lax.all_to_all(
        outgoing.reshape(n_experts, capacity, -1), "expert", split_axis=0, concat_axis=0, tiled=True
    )
    blocks = lax.all_to_all(
        received.reshape(n_slots, n_dp * piece), "dp", split_axis=1, concat_axis=0, tiled=True
    )
    if n_dp == 4 and n_tensor == 2 and gate_proj.shape[2] % (4 * CHUNK) == 0:
        expert_rows = experts(blocks, gate_proj[0], up_proj[0], down_proj[0])
    else:
        expert_rows = plain_experts(blocks, gate_proj, up_proj, down_proj)
    back = lax.all_to_all(expert_rows, "dp", split_axis=0, concat_axis=1, tiled=True)
    returned = lax.all_to_all(
        back.reshape(n_experts, capacity, -1), "expert", split_axis=0, concat_axis=0, tiled=True
    ).reshape(n_slots, -1)
    picked = jnp.take(returned, dest_slot, axis=0).astype(jnp.float32)
    picked = picked.reshape(n_tokens, TOPK, -1)
    mixed = jnp.sum(picked * route_weights[:, :, None], axis=1).astype(jnp.bfloat16)
    if n_dp % n_tensor == 0:
        mixed = lax.all_to_all(
            mixed.reshape(n_tokens, n_tensor, n_dp // n_tensor, 1, piece),
            "tensor", split_axis=1, concat_axis=3, tiled=True,
        )
        return mixed.reshape(n_tokens, part)
    whole = lax.all_gather(mixed.reshape(n_tokens, n_dp, 1, piece), "tensor", axis=2, tiled=True)
    whole = whole.reshape(n_tokens, n_tensor, part)
    return lax.dynamic_index_in_dim(whole, lax.axis_index("tensor"), 1, False)


def solution(mesh):
    placed = (
        P(("dp", "expert"), "tensor"),
        P(("dp", "expert"), None),
        P(("dp", "expert"), None),
        P("expert", "dp", "tensor"),
        P("expert", "dp", "tensor"),
        P("expert", "tensor", "dp"),
    )
    return jax.shard_map(
        shards, mesh=mesh, in_specs=placed, out_specs=P(("dp", "expert"), "tensor"), check_vma=False
    )
```

```python
import functools

import jax
import jax.numpy as jnp
from jax import lax
from jax.experimental import pallas as pl
from jax.experimental.pallas import tpu as pltpu
from jax.sharding import PartitionSpec as P

TOPK = 2
CHUNK = 256
MESH = pl.DeviceIdType.MESH


def kernel(
    n_chunks, x_ref, wg_ref, wu_ref, wd_ref, out_ref,
    xs, wt, wd, snd1, rcv1, snd2, rcv2, hid, keep, acc, ysnd, yrcv,
    w_sem, wd_sem, x_sem, y_sem, s1, r1, s2, r2, hs, hr,
):
    me, ex, core = lax.axis_index("dp"), lax.axis_index("expert"), lax.axis_index("tensor")
    mx, my = me % 2, me // 2
    xn, yn, diag = my * 2 + 1 - mx, (1 - my) * 2 + mx, 3 - me
    to_x, to_y, to_core = (xn, ex, core), (yn, ex, core), (me, ex, 1 - core)
    half = x_ref.shape[1]
    owned = n_chunks * CHUNK
    owners = (diag, diag, xn, yn, yn, xn, me, me)

    def weight(k, c, slot):
        src = wg_ref if k % 2 == 0 else wu_ref
        cols = pl.ds(pl.multiple_of(owners[k] * owned + c * CHUNK, CHUNK), CHUNK)
        return pltpu.make_async_copy(src.at[:, cols], wt.at[slot, k], w_sem.at[slot, k])

    def remote(src, dst, send, recv, to):
        return pltpu.make_async_remote_copy(
            src_ref=src, dst_ref=dst, send_sem=send, recv_sem=recv,
            device_id=to, device_id_type=MESH,
        )

    def first(c, k):
        return remote(snd1.at[c, k], rcv1.at[c, k], s1.at[c, k], r1.at[c, k],
                      to_x if k % 2 == 0 else to_y)

    def second(c, k):
        return remote(snd2.at[c, k], rcv2.at[c, k], s2.at[c, k], r2.at[c, k],
                      to_y if k == 0 else to_x)

    def spread(c, k):
        if k == 0:
            return remote(hid.at[c, 0], hid.at[c, 1], hs.at[c, 0], hr.at[c, 0], to_x)
        if k == 1:
            return remote(hid.at[c, 0], hid.at[c, 2], hs.at[c, 1], hr.at[c, 1], to_y)
        cols = pl.ds((k - 2) * (CHUNK // 2), CHUNK // 2)
        return remote(hid.at[c, k - 1, :, cols], hid.at[c, 3, :, cols], hs.at[c, k],
                      hr.at[c, k], to_y if k == 2 else to_x)

    down_copy = pltpu.make_async_copy(wd_ref, wd, wd_sem)
    for k in range(8):
        weight(k, 0, 0).start()
    barrier = pltpu.get_barrier_semaphore()
    for to in (to_x, to_y, to_core):
        pl.semaphore_signal(barrier, inc=1, device_id=to, device_id_type=MESH)
    pl.semaphore_wait(barrier, 3)
    x_copy = remote(x_ref, xs.at[core], x_sem.at[0], x_sem.at[1], to_core)
    x_copy.start()
    xs[core] = x_ref[...]
    acc[...] = jnp.zeros_like(acc)
    x_copy.wait()

    def product(slot, k):
        return jnp.dot(
            xs[0], wt[slot, k, :half, :], preferred_element_type=jnp.float32
        ) + jnp.dot(xs[1], wt[slot, k, half:, :], preferred_element_type=jnp.float32)

    def step(i, carry):
        @pl.when(i < n_chunks)
        def _():
            c = jnp.minimum(i, n_chunks - 1)
            slot = c % 2

            @pl.when(c + 1 < n_chunks)
            def _():
                for k in range(8):
                    weight(k, c + 1, 1 - slot).start()

            @pl.when(c == 0)
            def _():
                down_copy.start()

            for k in range(4):
                weight(k, c, slot).wait()
                snd1[c, k] = product(slot, k).astype(jnp.bfloat16)
                first(c, k).start()
            for k in range(4, 8):
                weight(k, c, slot).wait()
                keep[c % 3, k - 4] = product(slot, k)

        @pl.when((i >= 1) & (i < n_chunks + 1))
        def _():
            c = i - 1
            for k in range(2):
                first(c, k).wait_recv()
                snd2[c, k] = (keep[c % 3, k] + rcv1[c, k].astype(jnp.float32)).astype(jnp.bfloat16)
                second(c, k).start()

        @pl.when((i >= 3) & (i < n_chunks + 3))
        def _():
            c = i - 3
            for k in range(2):
                spread(c, k).wait_recv()
                spread(c, k + 2).start()

        @pl.when((i >= 2) & (i < n_chunks + 2))
        def _():
            c = i - 2
            first(c, 2).wait_recv()
            first(c, 3).wait_recv()
            second(c, 0).wait_recv()
            second(c, 1).wait_recv()
            gate = keep[c % 3, 2] + rcv1[c, 2].astype(jnp.float32) + rcv2[c, 0].astype(jnp.float32)
            up = keep[c % 3, 3] + rcv1[c, 3].astype(jnp.float32) + rcv2[c, 1].astype(jnp.float32)
            hid[c, 0] = (gate / (1.0 + jnp.exp(-gate)) * up).astype(jnp.bfloat16)
            spread(c, 0).start()
            spread(c, 1).start()

        @pl.when(i >= 4)
        def _():
            c = i - 4

            @pl.when(c == 0)
            def _():
                down_copy.wait()

            spread(c, 2).wait_recv()
            spread(c, 3).wait_recv()
            for n in range(0, acc.shape[1], 512):
                total = acc[:, n : n + 512]
                for s, owner in enumerate((me, xn, yn, diag)):
                    at = pl.ds(pl.multiple_of(owner * owned + c * CHUNK, CHUNK), CHUNK)
                    total += jnp.dot(
                        hid[c, s], wd[at, n : n + 512], preferred_element_type=jnp.float32
                    )
                acc[:, n : n + 512] = total

        return carry

    lax.fori_loop(0, n_chunks + 4, step, 0)
    ysnd[0] = acc[:, :half].astype(jnp.bfloat16)
    ysnd[1] = acc[:, half:].astype(jnp.bfloat16)
    y_copy = remote(ysnd.at[1 - core], yrcv, y_sem.at[0], y_sem.at[1], to_core)
    y_copy.start()

    def drain(c, carry):
        for k in range(4):
            first(c, k).wait_send()
            spread(c, k).wait_send()
        for k in range(2):
            second(c, k).wait_send()
        return carry

    lax.fori_loop(0, n_chunks, drain, 0)
    y_copy.wait()
    out_ref[...] = (ysnd[core].astype(jnp.float32) + yrcv[...].astype(jnp.float32)).astype(
        jnp.bfloat16
    )


def experts(blocks, gate_proj, up_proj, down_proj):
    rows, half = blocks.shape
    width, ff = gate_proj.shape
    n_chunks = ff // (4 * CHUNK)
    vmem = pl.BlockSpec(memory_space=pltpu.VMEM)
    hbm = pl.BlockSpec(memory_space=pl.ANY)
    bf, dma = jnp.bfloat16, pltpu.SemaphoreType.DMA
    return pl.pallas_call(
        functools.partial(kernel, n_chunks),
        out_shape=jax.ShapeDtypeStruct((rows, half), bf),
        in_specs=[vmem, hbm, hbm, hbm],
        out_specs=vmem,
        scratch_shapes=[
            pltpu.VMEM((2, rows, half), bf),
            pltpu.VMEM((2, 8, width, CHUNK), bf),
            pltpu.VMEM((ff, width), bf),
            pltpu.VMEM((n_chunks, 4, rows, CHUNK), bf),
            pltpu.VMEM((n_chunks, 4, rows, CHUNK), bf),
            pltpu.VMEM((n_chunks, 2, rows, CHUNK), bf),
            pltpu.VMEM((n_chunks, 2, rows, CHUNK), bf),
            pltpu.VMEM((n_chunks, 4, rows, CHUNK), bf),
            pltpu.VMEM((3, 4, rows, CHUNK), jnp.float32),
            pltpu.VMEM((rows, width), jnp.float32),
            pltpu.VMEM((2, rows, half), bf),
            pltpu.VMEM((rows, half), bf),
            dma((2, 8)), dma, dma((2,)), dma((2,)),
            dma((n_chunks, 4)), dma((n_chunks, 4)),
            dma((n_chunks, 2)), dma((n_chunks, 2)),
            dma((n_chunks, 4)), dma((n_chunks, 4)),
        ],
        compiler_params=pltpu.CompilerParams(
            collective_id=0, has_side_effects=True, vmem_limit_bytes=63 * 1024 * 1024
        ),
        cost_estimate=pl.CostEstimate(
            flops=6 * rows * width * ff, bytes_accessed=6 * width * ff,
            transcendentals=rows * ff // 4,
        ),
    )(blocks, gate_proj, up_proj, down_proj)


def plain_experts(blocks, gate_proj, up_proj, down_proj):
    rows = lax.all_gather(blocks, "tensor", axis=1, tiled=True)
    gate_part = jnp.dot(rows, gate_proj[0], preferred_element_type=jnp.float32)
    gate_sum = lax.psum_scatter(
        gate_part, "dp", scatter_dimension=0, tiled=True
    ).astype(jnp.float32)
    up_part = jnp.dot(rows, up_proj[0], preferred_element_type=jnp.float32)
    up_sum = lax.psum_scatter(
        up_part, "dp", scatter_dimension=0, tiled=True
    ).astype(jnp.float32)
    hidden = (jax.nn.silu(gate_sum) * up_sum).astype(jnp.bfloat16)
    hidden = lax.all_gather(hidden, "dp", axis=0, tiled=True)
    terms = jnp.dot(hidden, down_proj[0], preferred_element_type=jnp.float32)
    expert_rows = lax.psum_scatter(
        terms.astype(jnp.bfloat16), "tensor", scatter_dimension=1, tiled=True
    )
    return expert_rows


def shards(tokens, routes, route_weights, gate_proj, up_proj, down_proj):
    n_tokens, part = tokens.shape
    n_experts = lax.axis_size("expert") * gate_proj.shape[0]
    n_dp, n_tensor = lax.axis_size("dp"), lax.axis_size("tensor")
    capacity = min(n_tokens, n_tokens * TOPK // n_experts + 2)
    n_slots = n_experts * capacity
    width = part * n_tensor // n_dp
    piece = width // n_tensor
    if n_dp % n_tensor == 0:
        spread = lax.all_to_all(
            tokens.reshape(n_tokens, n_dp // n_tensor, n_tensor, piece),
            "tensor", split_axis=2, concat_axis=1, tiled=True,
        )
        spread = spread.reshape(n_tokens, n_dp * piece)
    else:
        whole = lax.all_gather(tokens, "tensor", axis=1, tiled=True)
        whole = whole.reshape(n_tokens, n_dp, n_tensor, piece)
        spread = lax.dynamic_index_in_dim(whole, lax.axis_index("tensor"), 2, False)
        spread = spread.reshape(n_tokens, n_dp * piece)
    flat_routes = routes.reshape(-1)
    one_hot = (flat_routes[:, None] == jnp.arange(n_experts, dtype=jnp.int32)[None, :]).astype(
        jnp.int32
    )
    earlier = jnp.cumsum(one_hot, axis=0) - one_hot
    slot_index = jnp.sum(earlier * one_hot, axis=1)
    dest_slot = flat_routes * capacity + slot_index
    slots = jnp.arange(n_slots, dtype=jnp.int32)
    dest = dest_slot.reshape(n_tokens, TOPK)
    select = sum(
        (dest[:, k][None, :] == slots[:, None]).astype(jnp.bfloat16) for k in range(TOPK)
    )
    outgoing = jnp.dot(select, spread, preferred_element_type=jnp.float32).astype(jnp.bfloat16)
    planes = ("dp", "expert")
    n_groups, lanes = n_dp * n_experts, 128 if piece % 128 == 0 else piece
    outgoing = outgoing.reshape(n_experts, capacity, n_dp, piece // lanes, lanes)
    outgoing = outgoing.transpose(2, 0, 3, 1, 4).reshape(n_groups, -1, lanes)
    received = lax.all_to_all(outgoing, planes, split_axis=0, concat_axis=0, tiled=True)
    received = received.reshape(n_groups, piece // lanes, capacity, lanes)
    blocks = received.transpose(0, 2, 1, 3).reshape(n_groups * capacity, piece)
    if n_dp == 4 and n_tensor == 2 and gate_proj.shape[2] % (4 * CHUNK) == 0:
        expert_rows = experts(blocks, gate_proj[0], up_proj[0], down_proj[0])
    else:
        expert_rows = plain_experts(blocks, gate_proj, up_proj, down_proj)
    leaving = expert_rows.reshape(n_groups, capacity, piece // lanes, lanes)
    leaving = leaving.transpose(0, 2, 1, 3).reshape(n_groups, -1, lanes)
    returned = lax.all_to_all(leaving, planes, split_axis=0, concat_axis=0, tiled=True)
    returned = returned.reshape(n_dp, n_experts, piece // lanes, capacity, lanes)
    returned = returned.transpose(1, 3, 0, 2, 4).reshape(n_slots, -1)
    picked = jnp.take(returned, dest_slot, axis=0).astype(jnp.float32)
    picked = picked.reshape(n_tokens, TOPK, -1)
    mixed = jnp.sum(picked * route_weights[:, :, None], axis=1).astype(jnp.bfloat16)
    if n_dp % n_tensor == 0:
        mixed = lax.all_to_all(
            mixed.reshape(n_tokens, n_tensor, n_dp // n_tensor, 1, piece),
            "tensor", split_axis=1, concat_axis=3, tiled=True,
        )
        return mixed.reshape(n_tokens, part)
    whole = lax.all_gather(mixed.reshape(n_tokens, n_dp, 1, piece), "tensor", axis=2, tiled=True)
    whole = whole.reshape(n_tokens, n_tensor, part)
    return lax.dynamic_index_in_dim(whole, lax.axis_index("tensor"), 1, False)


def solution(mesh):
    placed = (
        P(("dp", "expert"), "tensor"),
        P(("dp", "expert"), None),
        P(("dp", "expert"), None),
        P("expert", "dp", "tensor"),
        P("expert", "dp", "tensor"),
        P("expert", "tensor", "dp"),
    )
    return jax.shard_map(
        shards, mesh=mesh, in_specs=placed, out_specs=P(("dp", "expert"), "tensor"), check_vma=False
    )
```
